32 devices in a mesh: groups: 2 (over y), nodes: 16 (over z, x, core).
Axes of the slice: x: 2, y: 2, z: 4, core: 2. Of those that a mesh axis runs over, the one named last changes fastest.
Arguments:
- grid_feats: bfloat16 [32768, 1024], P(('groups', 'nodes')), parts along dimension 0, may hold values from -6 to 6
- mesh_feats: bfloat16 [4096, 1024], P(('groups', 'nodes')), parts along dimension 0, may hold values from -6 to 6
- mesh_cot: bfloat16 [4096, 1024], P(('groups', 'nodes')), parts along dimension 0, may hold values from -6 to 6
- w_src: bfloat16 [1024, 1024], replicated, may hold values from -0.1875 to 0.1875
- w_dst: bfloat16 [1024, 1024], replicated, may hold values from -0.1875 to 0.1875
- w_out: bfloat16 [1024, 1024], replicated, may hold values from -0.1875 to 0.1875
- edge_bias: float32 [1024], replicated, may hold values from -4 to 4
- tile_src: int32 [192], P(('groups', 'nodes')), parts along dimension 0, may hold values from 0 to 7
- tile_rows: int32 [192, 128], P(('groups', 'nodes')), parts along dimension 0, may hold values from 0 to 128, as said below
- tile_count: int32 [96], P(('groups', 'nodes')), parts along dimension 0, may hold values from 0 to 2, as said below
Outputs:
- mesh_out: bfloat16 [4096, 1024], P(('groups', 'nodes')), parts along dimension 0
- grid_grad: bfloat16 [32768, 1024], P(('groups', 'nodes')), parts along dimension 0
- mesh_grad: bfloat16 [4096, 1024], P(('groups', 'nodes')), parts along dimension 0
The draws below stay inside these ranges and needn't reach their ends.
There are 2 independent parts, one for each index of `groups`. The reference program is written for one: setup_inputs(seed, part) draws one part's arguments, and reference() takes and returns one part's arrays. A program takes and returns all parts, laid end to end along the dimension named above; an argument that names none is the same for every part. Nothing has to cross between parts.
Inputs may be any that keep to these rules, and one draw needn't show every extreme that they name: `tile_count`: tile slots of a device and destination beyond its count carry no edges. `tile_rows`: the value 128 marks a grid point of a tile without an edge.
All inputs are finite; a program needn't handle non-finite values.
Results may differ from the reference program's by a relative error of at most 0.0051.
Values may be sent and summed in bfloat16 or wider, within the bound.
A program may use at most 64 MiB of HBM per device.

```python
import jax
import jax.numpy as jnp
from jax import lax

D = 1024
E = 1024
BLK = 128
OFFS = 3
CAP = 2
GB_DEV = 8
GRID = 16384
MESH = 2048
TILES = 96
COUNTS = 48
N_NODES = 16


def draw_tile_src(key, part):
    key = jax.random.fold_in(key, 11)
    values = jax.random.randint(key, (TILES,), 0, GB_DEV, dtype=jnp.int32)
    return values.at[0].set(GB_DEV - 1).at[1].set(0)


def draw_tile_rows(key, part):
    key = jax.random.fold_in(key, 23)
    values = jax.random.randint(key, (TILES, BLK), 0, BLK + BLK // 8, dtype=jnp.int32)
    values = jnp.minimum(values, BLK)
    return values.at[0, 0].set(BLK).at[0, 1].set(0)


def draw_tile_count(key, part):
    key = jax.random.fold_in(key, 37)
    level_key, jitter_key = jax.random.split(key)
    level = jax.random.randint(level_key, (COUNTS // OFFS, 1), 0, CAP + 1, dtype=jnp.int32)
    jitter = jax.random.randint(jitter_key, (COUNTS // OFFS, OFFS), 0, 2, dtype=jnp.int32)
    counts = jnp.minimum(level + jitter, CAP).reshape(COUNTS)
    return counts.at[0].set(CAP).at[1].set(0)


def levels(own_key, extent, cuts, low, top_value):
    level = 1.0
    for position, blocks in cuts:
        heights = jax.random.uniform(jax.random.fold_in(jax.random.fold_in(own_key, 6), position), (blocks,), jnp.float32, low / len(cuts), top_value / len(cuts))
        level = level * jnp.repeat(jnp.exp(heights), extent[position] // blocks).reshape((-1,) + (1,) * (len(extent) - 1 - position))
    return level


def centred(stream_key, extent, spread, limit, cuts=(), held_as=jnp.bfloat16):
    entries = jax.random.normal(stream_key, extent, jnp.float32) * spread
    if len(cuts) > 0:
        entries = levels(stream_key, extent, cuts, -0.22, 0.18) * entries
    return jnp.clip(entries, min=-limit, max=limit).astype(held_as)


def setup_inputs(seed: int = 0, part: int = 0) -> dict:
    streams_of = jax.random.split(jax.random.key(seed), 11)
    part_splits = jax.random.split(jax.random.fold_in(streams_of[10], part), 11)
    grid_feats = centred(part_splits[0], (GRID, D), 1.0, 6.0, ((0, 16),))
    mesh_feats = centred(part_splits[1], (MESH, D), 1.0, 6.0, ((0, 16),))
    mesh_cot = centred(part_splits[2], (MESH, D), 1.0, 6.0, ((0, 16),))
    w_src = centred(streams_of[3], (D, E), D ** -0.5, 0.1875)
    w_dst = centred(streams_of[4], (D, E), D ** -0.5, 0.1875)
    w_out = centred(streams_of[5], (E, D), E ** -0.5, 0.1875)
    edge_bias = centred(streams_of[6], (E,), 1.0, 4.0, (), jnp.float32)
    tile_src = draw_tile_src(jax.random.fold_in(jax.random.fold_in(streams_of[10], part), 71), part)
    tile_rows = draw_tile_rows(jax.random.fold_in(jax.random.fold_in(streams_of[10], part), 71), part)
    tile_count = draw_tile_count(jax.random.fold_in(jax.random.fold_in(streams_of[10], part), 71), part)
    return dict(grid_feats=grid_feats, mesh_feats=mesh_feats, mesh_cot=mesh_cot, w_src=w_src, w_dst=w_dst, w_out=w_out, edge_bias=edge_bias, tile_src=tile_src, tile_rows=tile_rows, tile_count=tile_count)


def silu_slope(value):
    sig = jax.nn.sigmoid(value)
    return sig * (1.0 + value * (1.0 - sig))


def reference(grid_feats, mesh_feats, mesh_cot, w_src, w_dst, w_out, edge_bias, tile_src, tile_rows, tile_count):
    x_all = grid_feats.reshape(N_NODES, GB_DEV, BLK, D)
    h_proj = jnp.dot(mesh_feats, w_dst, preferred_element_type=jnp.float32)
    g_proj = lax.dot_general(mesh_cot, w_out, (((1,), (1,)), ((), ())), preferred_element_type=jnp.float32)
    src_all = tile_src.reshape(N_NODES, OFFS * CAP)
    rows_all = tile_rows.reshape(N_NODES, OFFS * CAP, BLK)
    count_all = tile_count.reshape(N_NODES, OFFS)
    slot_off = jnp.repeat(jnp.arange(OFFS, dtype=jnp.int32), CAP)
    slot_pos = jnp.tile(jnp.arange(CAP, dtype=jnp.int32), OFFS)

    def one_device(carry, device):
        mesh_sum, pre_sum = carry
        x_dev = x_all[device]
        sources = src_all[device]
        rows = rows_all[device]
        counts = count_all[device]
        alive = (slot_pos < counts[slot_off])[:, None] & (rows < BLK)
        dest = (device + slot_off - OFFS // 2) % N_NODES
        flat = (dest[:, None] * BLK + jnp.minimum(rows, BLK - 1)).reshape(-1).astype(jnp.int32)
        tile_feats = x_dev[sources].reshape(-1, D)
        edge_mask = alive.reshape(-1, 1).astype(jnp.float32)
        pre_act = jnp.dot(tile_feats, w_src, preferred_element_type=jnp.float32) + edge_bias + h_proj[flat]
        hidden_act = jax.nn.silu(pre_act).astype(jnp.bfloat16)
        message = jnp.dot(hidden_act, w_out, preferred_element_type=jnp.float32) * edge_mask
        pre_grad = (g_proj[flat] * silu_slope(pre_act) * edge_mask).astype(jnp.bfloat16)
        feat_grad = lax.dot_general(pre_grad, w_src, (((1,), (1,)), ((), ())), preferred_element_type=jnp.float32)
        block_grad = jnp.zeros((GB_DEV, BLK, D), jnp.float32).at[sources].add(feat_grad.reshape(OFFS * CAP, BLK, D))
        mesh_sum = mesh_sum.at[flat].add(message)
        pre_sum = pre_sum.at[flat].add(pre_grad.astype(jnp.float32))
        return (mesh_sum, pre_sum), block_grad.astype(jnp.bfloat16).reshape(GB_DEV * BLK, D)

    start = (jnp.zeros((MESH, D), jnp.float32), jnp.zeros((MESH, E), jnp.float32))
    (mesh_sum, pre_sum), grads = lax.scan(one_device, start, jnp.arange(N_NODES, dtype=jnp.int32))
    mesh_out = (mesh_feats.astype(jnp.float32) + mesh_sum).astype(jnp.bfloat16)
    pre_round = pre_sum.astype(jnp.bfloat16)
    mesh_grad = (mesh_cot.astype(jnp.float32) + lax.dot_general(pre_round, w_dst, (((1,), (1,)), ((), ())), preferred_element_type=jnp.float32)).astype(jnp.bfloat16)
    grid_grad = grads.reshape(GRID, D)
    return mesh_out, grid_grad, mesh_grad
```

```python
import functools

import jax
import jax.numpy as jnp
from jax import lax
from jax.experimental import pallas as pl
from jax.experimental.pallas import tpu as pltpu
from jax.sharding import PartitionSpec as P

NODES = "nodes"
COLS = 256
F32 = jnp.float32
BF16 = jnp.bfloat16


def nt_dot(a, b):
    return lax.dot_general(a, b, (((1,), (1,)), ((), ())), preferred_element_type=F32)


def nn_dot(a, b):
    return jnp.dot(a, b, preferred_element_type=F32)


def high_low(value):
    high = value.astype(BF16)
    low = (value - high.astype(F32)).astype(BF16)
    return jnp.concatenate([high, low], axis=0)


def kernel(
    n,
    tile_src,
    tile_count,
    rows_ref,
    bias_ref,
    x_hbm,
    feats_hbm,
    cot_hbm,
    wsrc_hbm,
    wdst_hbm,
    wout_hbm,
    mesh_out,
    grid_grad,
    mesh_grad,
    x_v,
    wsrc,
    wdst,
    wout,
    feats,
    cot,
    xt,
    pre,
    pg,
    spread,
    pick,
    s_own,
    p_own,
    s_send,
    p_send,
    feats_in,
    cot_in,
    s_in,
    p_in,
    gt,
    gg,
    mo,
    mg,
    load_sem,
    store_sem,
    send_sem,
    recv_sem,
):
    blk = rows_ref.shape[1]
    slots = rows_ref.shape[0]
    offs = tile_count.shape[0]
    cap = slots // offs
    own = offs // 2
    width = x_v.shape[1]
    hidden_width = wsrc.shape[1]
    grid_blocks = x_v.shape[0] // blk
    per = cap * blk

    me = lax.axis_index(NODES)
    right = lax.rem(me + 1, n)
    left = lax.rem(me + n - 1, n)

    def load(i, src, dst):
        copy = pltpu.make_async_copy(src, dst, load_sem.at[i])
        copy.start()
        return copy

    load_x = load(0, x_hbm, x_v)
    load_wsrc = load(1, wsrc_hbm, wsrc)
    load_feats = load(2, feats_hbm, feats)
    load_wdst = load(3, wdst_hbm, wdst)
    load_cot = load(4, cot_hbm, cot)
    load_wout = load(5, wout_hbm, wout)

    barrier = pltpu.get_barrier_semaphore()
    for neighbour in (left, right):
        pl.semaphore_signal(
            barrier, inc=1, device_id={NODES: neighbour}, device_id_type=pl.DeviceIdType.MESH
        )
    pl.semaphore_wait(barrier, 2)

    def send(kind, way, src, landing):
        return pltpu.make_async_remote_copy(
            src_ref=src,
            dst_ref=landing.at[way],
            send_sem=send_sem.at[kind, way],
            recv_sem=recv_sem.at[kind, way],
            device_id={NODES: right if way == 0 else left},
            device_id_type=pl.DeviceIdType.MESH,
        )

    feat_sends = [send(0, way, feats_hbm, feats_in) for way in range(2)]
    cot_sends = [send(1, way, cot_hbm, cot_in) for way in range(2)]
    s_sends = [send(2, way, s_send.at[way], s_in) for way in range(2)]
    p_sends = [send(3, way, p_send.at[way], p_in) for way in range(2)]
    for copy in feat_sends:
        copy.start()

    row_id = lax.broadcasted_iota(jnp.int32, (blk, blk), 0)
    for t in range(slots):
        o, c = t // cap, t % cap
        count = jnp.full((1, blk), tile_count[o], jnp.int32)
        rows = jnp.where(count > c, rows_ref[pl.ds(t, 1), :], blk)
        hit = jnp.where(row_id == rows, 1.0, 0.0).astype(F32)
        spread[o, :, c * blk : (c + 1) * blk] = hit.astype(BF16)
        turned = hit.T.astype(BF16)
        pick[t * blk : (t + 1) * blk, :blk] = turned
        pick[t * blk : (t + 1) * blk, blk:] = turned

    def chunk(i):
        return pl.ds(pl.multiple_of(i * COLS, COLS), COLS)

    def share(t, b):
        source = jnp.full((1, COLS), tile_src[t], jnp.int32)
        return jnp.where(source == b, 1.0, 0.0).astype(F32)

    load_x.wait()

    @pl.loop(0, width // COLS)
    def _(i):
        at = chunk(i)
        for t in range(slots):
            tile = share(t, 0).astype(BF16) * x_v[:blk, at]
            for b in range(1, grid_blocks):
                tile += share(t, b).astype(BF16) * x_v[b * blk : (b + 1) * blk, at]
            xt[t * blk : (t + 1) * blk, at] = tile

    load_wsrc.wait()

    @pl.loop(0, hidden_width // COLS)
    def _(i):
        at = chunk(i)
        pre[:, at] = nn_dot(xt[...], wsrc[:, at]) + bias_ref[:, at]

    def hidden_part(o, feats_ref, s_ref):
        lines = slice(o * per, (o + 1) * per)

        @pl.loop(0, hidden_width // COLS)
        def _(i):
            at = chunk(i)
            h = nn_dot(feats_ref[...], wdst[:, at])
            act = pre[lines, at] + nn_dot(pick[lines, :], high_low(h))
            sig = 0.5 * jnp.tanh(0.5 * act) + 0.5
            hidden = act * sig
            pre[lines, at] = sig + hidden * (1.0 - sig)
            s_ref[:, at] = nn_dot(spread[o], hidden.astype(BF16)).astype(s_ref.dtype)

    def grad_part(o, cot_ref, p_ref):
        lines = slice(o * per, (o + 1) * per)

        @pl.loop(0, hidden_width // COLS)
        def _(i):
            at = chunk(i)
            g = nt_dot(cot_ref[...], wout[at, :])
            grad = (nn_dot(pick[lines, :], high_low(g)) * pre[lines, at]).astype(BF16)
            pg[lines, at] = grad
            p_ref[:, at] = nn_dot(spread[o], grad).astype(p_ref.dtype)

    load_feats.wait()
    load_wdst.wait()
    hidden_part(own, feats, s_own)

    for way in range(2):
        feat_sends[way].wait_send()
        cot_sends[way].start()

    feat_sends[0].wait_recv()
    hidden_part(own - 1, feats_in.at[0], s_send.at[1])
    feat_sends[1].wait_recv()
    hidden_part(own + 1, feats_in.at[1], s_send.at[0])

    load_cot.wait()
    load_wout.wait()
    grad_part(own, cot, p_own)

    for way in range(2):
        cot_sends[way].wait_send()
        s_sends[way].start()

    cot_sends[0].wait_recv()
    grad_part(own - 1, cot_in.at[0], p_send.at[1])
    cot_sends[1].wait_recv()
    grad_part(own + 1, cot_in.at[1], p_send.at[0])

    for way in range(2):
        p_sends[way].start()

    @pl.loop(0, width // COLS)
    def _(i):
        at = chunk(i)
        gt[...] = nt_dot(pg[...], wsrc[at, :])
        for b in range(grid_blocks):
            total = share(0, b) * gt[:blk, :]
            for t in range(1, slots):
                total += share(t, b) * gt[t * blk : (t + 1) * blk, :]
            gg[b * blk : (b + 1) * blk, at] = total.astype(BF16)

    store_grid = pltpu.make_async_copy(gg, grid_grad, store_sem.at[0])
    store_grid.start()

    for way in range(2):
        s_sends[way].wait_recv()
    s_all = high_low(s_own[...] + s_in[0].astype(F32) + s_in[1].astype(F32))
    xt[: 2 * blk, :] = s_all

    @pl.loop(0, width // COLS)
    def _(i):
        at = chunk(i)
        both = nn_dot(xt[: 2 * blk, :], wout[:, at])
        mo[:, at] = (feats[:, at].astype(F32) + both[:blk] + both[blk:]).astype(BF16)

    store_mesh = pltpu.make_async_copy(mo, mesh_out, store_sem.at[1])
    store_mesh.start()

    for way in range(2):
        p_sends[way].wait_recv()
    xt[:blk, :] = (p_own[...] + p_in[0].astype(F32) + p_in[1].astype(F32)).astype(BF16)

    @pl.loop(0, width // COLS)
    def _(i):
        at = chunk(i)
        mg[:, at] = (cot[:, at].astype(F32) + nt_dot(xt[:blk, :], wdst[at, :])).astype(BF16)

    store_cot = pltpu.make_async_copy(mg, mesh_grad, store_sem.at[2])
    store_cot.start()
    for way in range(2):
        s_sends[way].wait_send()
        p_sends[way].wait_send()
    store_grid.wait()
    store_mesh.wait()
    store_cot.wait()


def local(
    grid_feats,
    mesh_feats,
    mesh_cot,
    w_src,
    w_dst,
    w_out,
    edge_bias,
    tile_src,
    tile_rows,
    tile_count,
):
    n = lax.axis_size(NODES)
    slots, blk = tile_rows.shape
    width = grid_feats.shape[1]
    hid = w_src.shape[1]
    offs = tile_count.shape[0]
    cap = slots // offs
    anywhere = pl.BlockSpec(memory_space=pl.ANY)
    outside = pl.BlockSpec(memory_space=pltpu.HBM)
    scalar = pl.BlockSpec(memory_space=pltpu.SMEM)
    vector = pl.BlockSpec(memory_space=pltpu.VMEM)
    flops = 2 * width * hid * (2 * slots * blk + 8 * blk)
    return pl.pallas_call(
        functools.partial(kernel, n),
        out_shape=(
            jax.ShapeDtypeStruct(mesh_feats.shape, BF16),
            jax.ShapeDtypeStruct(grid_feats.shape, BF16),
            jax.ShapeDtypeStruct(mesh_cot.shape, BF16),
        ),
        in_specs=[scalar, scalar, vector, vector] + [outside] * 6,
        out_specs=(anywhere, anywhere, anywhere),
        scratch_shapes=[
            pltpu.VMEM(grid_feats.shape, BF16),
            pltpu.VMEM(w_src.shape, BF16),
            pltpu.VMEM(w_dst.shape, BF16),
            pltpu.VMEM(w_out.shape, BF16),
            pltpu.VMEM((blk, width), BF16),
            pltpu.VMEM((blk, width), BF16),
            pltpu.VMEM((slots * blk, width), BF16),
            pltpu.VMEM((slots * blk, hid), F32),
            pltpu.VMEM((slots * blk, hid), BF16),
            pltpu.VMEM((offs, blk, cap * blk), BF16),
            pltpu.VMEM((slots * blk, 2 * blk), BF16),
            pltpu.VMEM((blk, hid), F32),
            pltpu.VMEM((blk, hid), F32),
            pltpu.VMEM((2, blk, hid), BF16),
            pltpu.VMEM((2, blk, hid), BF16),
            pltpu.VMEM((2, blk, width), BF16),
            pltpu.VMEM((2, blk, width), BF16),
            pltpu.VMEM((2, blk, hid), BF16),
            pltpu.VMEM((2, blk, hid), BF16),
            pltpu.VMEM((slots * blk, COLS), F32),
            pltpu.VMEM(grid_feats.shape, BF16),
            pltpu.VMEM((blk, width), BF16),
            pltpu.VMEM((blk, width), BF16),
            pltpu.SemaphoreType.DMA((6,)),
            pltpu.SemaphoreType.DMA((3,)),
            pltpu.SemaphoreType.DMA((4, 2)),
            pltpu.SemaphoreType.DMA((4, 2)),
        ],
        compiler_params=pltpu.CompilerParams(
            collective_id=0, has_side_effects=True, vmem_limit_bytes=44 * 1024 * 1024
        ),
        cost_estimate=pl.CostEstimate(
            flops=flops, bytes_accessed=12 * 1024 * 1024, transcendentals=slots * blk * hid
        ),
    )(
        tile_src,
        tile_count,
        tile_rows,
        edge_bias.reshape(1, hid),
        grid_feats,
        mesh_feats,
        mesh_cot,
        w_src,
        w_dst,
        w_out,
    )


def solution(mesh):
    both = P(("groups", NODES))
    wide = P(("groups", NODES), None)
    return jax.shard_map(
        local,
        mesh=mesh,
        in_specs=(wide, wide, wide, P(), P(), P(), P(), both, wide, both),
        out_specs=(wide, wide, wide),
        check_vma=False,
    )
```

```python
import functools

import jax
import jax.numpy as jnp
from jax import lax
from jax.experimental import pallas as pl
from jax.experimental.pallas import tpu as pltpu
from jax.sharding import PartitionSpec as P

NODES = "nodes"
COLS = 256
PIECES = 8
F32 = jnp.float32
BF16 = jnp.bfloat16


def nt_dot(a, b):
    return lax.dot_general(a, b, (((1,), (1,)), ((), ())), preferred_element_type=F32)


def nn_dot(a, b):
    return jnp.dot(a, b, preferred_element_type=F32)


def high_low(value):
    high = value.astype(BF16)
    low = (value - high.astype(F32)).astype(BF16)
    return jnp.concatenate([high, low], axis=0)


def kernel(
    n,
    tile_src,
    tile_count,
    rows_ref,
    bias_ref,
    x_hbm,
    feats_hbm,
    cot_hbm,
    wsrc_hbm,
    wdst_hbm,
    wout_hbm,
    mesh_out,
    grid_grad,
    mesh_grad,
    x_v,
    wsrc,
    wdst,
    wout,
    feats,
    cot,
    xt,
    pre,
    pg,
    spread,
    pick,
    s_own,
    p_own,
    s_send,
    p_send,
    feats_in,
    cot_in,
    s_in,
    p_in,
    gt,
    gg,
    mo,
    mg,
    load_sem,
    store_sem,
    send_sem,
    recv_sem,
):
    blk = rows_ref.shape[1]
    slots = rows_ref.shape[0]
    offs = tile_count.shape[0]
    cap = slots // offs
    own = offs // 2
    width = x_v.shape[1]
    hidden_width = wsrc.shape[1]
    grid_blocks = x_v.shape[0] // blk
    per = cap * blk

    me = lax.axis_index(NODES)
    right = lax.rem(me + 1, n)
    left = lax.rem(me + n - 1, n)

    def load(i, src, dst):
        copy = pltpu.make_async_copy(src, dst, load_sem.at[i])
        copy.start()
        return copy

    load_x = load(0, x_hbm, x_v)
    load_wsrc = load(1, wsrc_hbm, wsrc)
    load_feats = load(2, feats_hbm, feats)
    load_wdst = load(3, wdst_hbm, wdst)
    load_cot = load(4, cot_hbm, cot)
    load_wout = load(5, wout_hbm, wout)

    barrier = pltpu.get_barrier_semaphore()
    for neighbour in (left, right):
        pl.semaphore_signal(
            barrier, inc=1, device_id={NODES: neighbour}, device_id_type=pl.DeviceIdType.MESH
        )
    pl.semaphore_wait(barrier, 2)

    def send(kind, way, src, landing):
        return pltpu.make_async_remote_copy(
            src_ref=src,
            dst_ref=landing.at[pl.ds(way * blk, blk)],
            send_sem=send_sem.at[kind, way],
            recv_sem=recv_sem.at[kind, way],
            device_id={NODES: right if way == 0 else left},
            device_id_type=pl.DeviceIdType.MESH,
        )

    feat_sends = [send(0, way, feats_hbm, feats_in) for way in range(2)]
    cot_sends = [send(1, way, cot_hbm, cot_in) for way in range(2)]
    s_sends = [send(2, way, s_send.at[pl.ds(way * blk, blk)], s_in) for way in range(2)]
    p_sends = [send(3, way, p_send.at[pl.ds(way * blk, blk)], p_in) for way in range(2)]
    for copy in feat_sends:
        copy.start()

    row_id = lax.broadcasted_iota(jnp.int32, (blk, blk), 0)
    for t in range(slots):
        o, c = t // cap, t % cap
        count = jnp.full((1, blk), tile_count[o], jnp.int32)
        rows = jnp.where(count > c, rows_ref[pl.ds(t, 1), :], blk)
        hit = jnp.where(row_id == rows, 1.0, 0.0).astype(F32)
        spread[o, :, c * blk : (c + 1) * blk] = hit.astype(BF16)
        turned = hit.T.astype(BF16)
        pick[t * blk : (t + 1) * blk, :blk] = turned
        pick[t * blk : (t + 1) * blk, blk:] = turned

    def chunks(total):
        return [slice(i, i + COLS) for i in range(0, total, COLS)]

    def share(t, b):
        source = jnp.full((1, COLS), tile_src[t], jnp.int32)
        return jnp.where(source == b, 1.0, 0.0).astype(F32)

    load_x.wait()

    for at in chunks(width):
        for t in range(slots):
            tile = share(t, 0).astype(BF16) * x_v[:blk, at]
            for b in range(1, grid_blocks):
                tile += share(t, b).astype(BF16) * x_v[b * blk : (b + 1) * blk, at]
            xt[t * blk : (t + 1) * blk, at] = tile

    load_wsrc.wait()

    for at in chunks(hidden_width):
        pre[:, at] = nn_dot(xt[...], wsrc[:, at]) + bias_ref[:, at]

    def hidden_part(dests, feats_ref, s_ref):
        for at in chunks(hidden_width):
            h = nn_dot(feats_ref[...], wdst[:, at])
            for k, o in enumerate(dests):
                lines = slice(o * per, (o + 1) * per)
                act = pre[lines, at] + nn_dot(pick[lines, :], high_low(h[k * blk : (k + 1) * blk]))
                sig = 0.5 * jnp.tanh(0.5 * act) + 0.5
                hidden = act * sig
                pre[lines, at] = sig + hidden * (1.0 - sig)
                back = len(dests) - 1 - k
                s_ref[back * blk : (back + 1) * blk, at] = nn_dot(
                    spread[o], hidden.astype(BF16)
                ).astype(s_ref.dtype)

    def grad_part(dests, cot_ref, p_ref):
        for at in chunks(hidden_width):
            g = nt_dot(cot_ref[...], wout[at, :])
            for k, o in enumerate(dests):
                lines = slice(o * per, (o + 1) * per)
                picked = nn_dot(pick[lines, :], high_low(g[k * blk : (k + 1) * blk]))
                grad = (picked * pre[lines, at]).astype(BF16)
                pg[lines, at] = grad
                back = len(dests) - 1 - k
                p_ref[back * blk : (back + 1) * blk, at] = nn_dot(spread[o], grad).astype(
                    p_ref.dtype
                )

    load_feats.wait()
    load_wdst.wait()
    hidden_part((own,), feats, s_own)
    for way in range(2):
        feat_sends[way].wait_send()
        cot_sends[way].start()
    load_cot.wait()
    load_wout.wait()
    grad_part((own,), cot, p_own)


    for way in range(2):
        feat_sends[way].wait_recv()
    hidden_part((own - 1, own + 1), feats_in, s_send)

    for way in range(2):
        s_sends[way].start()

    for way in range(2):
        cot_sends[way].wait_recv()
    grad_part((own - 1, own + 1), cot_in, p_send)

    for way in range(2):
        p_sends[way].start()

    for at in chunks(width):
        gt[...] = nt_dot(pg[...], wsrc[at, :])
        for b in range(grid_blocks):
            total = share(0, b) * gt[:blk, :]
            for t in range(1, slots):
                total += share(t, b) * gt[t * blk : (t + 1) * blk, :]
            gg[b * blk : (b + 1) * blk, at] = total.astype(BF16)

    store_grid = pltpu.make_async_copy(gg, grid_grad, store_sem.at[0])
    store_grid.start()

    for way in range(2):
        s_sends[way].wait_recv()
    s_all = high_low(s_own[...] + s_in[:blk].astype(F32) + s_in[blk:].astype(F32))
    xt[: 2 * blk, :] = s_all

    for at in chunks(width):
        both = nn_dot(xt[: 2 * blk, :], wout[:, at])
        mo[:, at] = (feats[:, at].astype(F32) + both[:blk] + both[blk:]).astype(BF16)

    store_mesh = pltpu.make_async_copy(mo, mesh_out, store_sem.at[1])
    store_mesh.start()

    for way in range(2):
        p_sends[way].wait_recv()
    xt[:blk, :] = (p_own[...] + p_in[:blk].astype(F32) + p_in[blk:].astype(F32)).astype(BF16)

    for at in chunks(width):
        mg[:, at] = (cot[:, at].astype(F32) + nt_dot(xt[:blk, :], wdst[at, :])).astype(BF16)

    store_cot = pltpu.make_async_copy(mg, mesh_grad, store_sem.at[2])
    store_cot.start()
    for way in range(2):
        cot_sends[way].wait_send()
        s_sends[way].wait_send()
        p_sends[way].wait_send()
    store_grid.wait()
    store_mesh.wait()
    store_cot.wait()


def local(
    grid_feats,
    mesh_feats,
    mesh_cot,
    w_src,
    w_dst,
    w_out,
    edge_bias,
    tile_src,
    tile_rows,
    tile_count,
):
    n = lax.axis_size(NODES)
    slots, blk = tile_rows.shape
    width = grid_feats.shape[1]
    hid = w_src.shape[1]
    offs = tile_count.shape[0]
    cap = slots // offs
    anywhere = pl.BlockSpec(memory_space=pl.ANY)
    outside = pl.BlockSpec(memory_space=pltpu.HBM)
    scalar = pl.BlockSpec(memory_space=pltpu.SMEM)
    vector = pl.BlockSpec(memory_space=pltpu.VMEM)
    flops = 2 * width * hid * (2 * slots * blk + 8 * blk)
    outs = pl.pallas_call(
        functools.partial(kernel, n),
        out_shape=(
            jax.ShapeDtypeStruct(mesh_feats.shape, BF16),
            jax.ShapeDtypeStruct(grid_feats.shape, BF16),
            jax.ShapeDtypeStruct(mesh_cot.shape, BF16),
        ),
        in_specs=[scalar, scalar, vector, vector] + [outside] * 6,
        out_specs=(anywhere, anywhere, anywhere),
        scratch_shapes=[
            pltpu.VMEM(grid_feats.shape, BF16),
            pltpu.VMEM(w_src.shape, BF16),
            pltpu.VMEM(w_dst.shape, BF16),
            pltpu.VMEM(w_out.shape, BF16),
            pltpu.VMEM((blk, width), BF16),
            pltpu.VMEM((blk, width), BF16),
            pltpu.VMEM((slots * blk, width), BF16),
            pltpu.VMEM((slots * blk, hid), F32),
            pltpu.VMEM((slots * blk, hid), BF16),
            pltpu.VMEM((offs, blk, cap * blk), BF16),
            pltpu.VMEM((slots * blk, 2 * blk), BF16),
            pltpu.VMEM((blk, hid), F32),
            pltpu.VMEM((blk, hid), F32),
            pltpu.VMEM((2 * blk, hid), BF16),
            pltpu.VMEM((2 * blk, hid), BF16),
            pltpu.VMEM((2 * blk, width), BF16),
            pltpu.VMEM((2 * blk, width), BF16),
            pltpu.VMEM((2 * blk, hid), BF16),
            pltpu.VMEM((2 * blk, hid), BF16),
            pltpu.VMEM((slots * blk, COLS), F32),
            pltpu.VMEM(grid_feats.shape, BF16),
            pltpu.VMEM((blk, width), BF16),
            pltpu.VMEM((blk, width), BF16),
            pltpu.SemaphoreType.DMA((6,)),
            pltpu.SemaphoreType.DMA((3,)),
            pltpu.SemaphoreType.DMA((4, 2)),
            pltpu.SemaphoreType.DMA((4, 2)),
        ],
        compiler_params=pltpu.CompilerParams(
            collective_id=0, has_side_effects=True, vmem_limit_bytes=63 * 1024 * 1024
        ),
        cost_estimate=pl.CostEstimate(
            flops=flops, bytes_accessed=12 * 1024 * 1024, transcendentals=slots * blk * hid
        ),
    )(
        tile_src,
        tile_count,
        tile_rows,
        edge_bias.reshape(1, hid),
        grid_feats,
        mesh_feats,
        mesh_cot,
        w_src,
        w_dst,
        w_out,
    )
    return pl.pallas_call(
        copy_out,
        out_shape=tuple(jax.ShapeDtypeStruct(o.shape, o.dtype) for o in outs),
        in_specs=[anywhere] * 3,
        out_specs=(anywhere,) * 3,
        scratch_shapes=[pltpu.VMEM(o.shape, o.dtype) for o in outs]
        + [pltpu.SemaphoreType.DMA((3, PIECES))] * 2,
        compiler_params=pltpu.CompilerParams(vmem_limit_bytes=63 * 1024 * 1024),
        cost_estimate=pl.CostEstimate(flops=0, bytes_accessed=5 * 1024 * 1024, transcendentals=0),
    )(*outs)


def copy_out(*refs):
    held, in_sem, out_sem = refs[6:9], refs[9], refs[10]
    parts = []
    for k in range(3):
        rows = refs[k].shape[0] // PIECES
        for j in range(PIECES):
            part = pl.ds(j * rows, rows)
            parts.append(
                (
                    pltpu.make_async_copy(refs[k].at[part], held[k].at[part], in_sem.at[k, j]),
                    pltpu.make_async_copy(held[k].at[part], refs[3 + k].at[part], out_sem.at[k, j]),
                )
            )
    for arrive, _ in parts:
        arrive.start()
    for arrive, leave in parts:
        arrive.wait()
        leave.start()
    for _, leave in parts:
        leave.wait()


def solution(mesh):
    both = P(("groups", NODES))
    wide = P(("groups", NODES), None)
    return jax.shard_map(
        local,
        mesh=mesh,
        in_specs=(wide, wide, wide, P(), P(), P(), P(), both, wide, both),
        out_specs=(wide, wide, wide),
        check_vma=False,
    )
```
